128 devices in a mesh: dp: 4 (over y_hi, core), seq: 32 (over y_lo, z, x).
Axes of the slice: x: 4, y: 4 (y_hi: 2, y_lo: 2; y = y_hi * 2 + y_lo), z: 4, core: 2. Of those that a mesh axis runs over, the one named last changes fastest.
Arguments:
- clip: bfloat16 [256, 512, 1152], P(('dp', 'seq')), parts along dimension 0, may hold values from -6 to 6
- modulation: float32 [24, 1152], P('dp'), parts along dimension 0, may hold values from -0.5 to 1.5
- w_qkv_s: bfloat16 [1152, 3456], replicated, may hold values from -1 to 1, as said below
- w_out_s: bfloat16 [1152, 1152], replicated, may hold values from -0.1875 to 0.1875
- w_qkv_t: bfloat16 [1152, 3456], replicated, may hold values from -1 to 1, as said below
- w_out_t: bfloat16 [1152, 1152], replicated, may hold values from -0.1875 to 0.1875
Outputs:
- blocks_out: bfloat16 [256, 512, 1152], P(('dp', 'seq')), parts along dimension 0
The draws below stay inside these ranges and needn't reach their ends.
There are 4 independent parts, one for each index of `dp`. The reference program is written for one: setup_inputs(seed, part) draws one part's arguments, and reference() takes and returns one part's arrays. A program takes and returns all parts, laid end to end along the dimension named above; an argument that names none is the same for every part. Nothing has to cross between parts.
Inputs may be any that keep to these rules, and one draw needn't show every extreme that they name: `w_qkv_s`: entries of order 1152**-0.5 times a few. `w_qkv_t`: entries of order 1152**-0.5 times a few.
All inputs are finite; a program needn't handle non-finite values.
Results may differ from the reference program's by a relative error of at most 0.03.
The reference program's roundings to bfloat16 on the way (of `modulated`, `qkv`, `weights`, `attended` and `spatial`) count: a program that leaves them out, or rounds other values in their place, can miss the bound.
Values may be sent and summed in bfloat16 or wider, within the bound.
No kernel may reach another device: no remote copies, remote signals or barrier semaphores. Data moves between devices by JAX's collectives and lax.ppermute only.
A program may use at most 192 MiB of HBM per device.

```python
import jax
import jax.numpy as jnp
from jax import lax

D = 1152
H = 16
P_SIZE = 512
FRAMES = 64


def qkv_matrix(key, top):
    values = jax.random.normal(key, (D, 3 * D), jnp.float32) * D ** (-0.5)
    heads = jax.random.uniform(jax.random.fold_in(key, 5), (H,), jnp.float32, 1.0, top)
    column = jnp.repeat(heads, D // H)
    factor = jnp.concatenate([column, column, jnp.ones((D,), jnp.float32)])
    return jnp.clip(values * factor, -1.0, 1.0)


def draw_w_qkv_s(key, part):
    key = jax.random.fold_in(key, 11)
    return qkv_matrix(key, 1.5).astype(jnp.bfloat16)


def draw_w_qkv_t(key, part):
    key = jax.random.fold_in(key, 23)
    return qkv_matrix(key, 1.5).astype(jnp.bfloat16)


def shard_levels(rng, extent, cuts, low, largest):
    gain, own = 1.0, jax.random.fold_in(rng, 6)
    for axis_at, blocks in cuts:
        heights = jnp.exp(jax.random.uniform(jax.random.fold_in(own, axis_at), (blocks,), jnp.float32, low / len(cuts), largest / len(cuts)))
        gain = gain * jnp.repeat(heights, extent[axis_at] // blocks).reshape([-1 if axis == axis_at else 1 for axis in range(len(extent))])
    return gain


def normal_values(rng, dims, scale, bound, cuts=(), held_as=jnp.bfloat16):
    array = jax.random.normal(rng, dims, jnp.float32) * scale
    if len(cuts) > 0:
        array = shard_levels(rng, dims, cuts, -0.22, 0.18) * array
    return jnp.clip(array, min=-bound, max=bound).astype(held_as)


def setup_inputs(seed: int = 0, part: int = 0) -> dict:
    key_list = jax.random.split(jax.random.key(seed), 7)
    part_keys = jax.random.split(jax.random.fold_in(key_list[6], part), 7)
    return {
        "clip": normal_values(part_keys[0], (FRAMES, P_SIZE, D), 1.0, 6.0, ((0, 32),)),
        "modulation": jnp.clip(jax.random.uniform(part_keys[1], (6, D), jnp.float32, -0.5, 1.5), -0.5, 1.5),
        "w_qkv_s": draw_w_qkv_s(jax.random.fold_in(key_list[6], 71), part),
        "w_out_s": normal_values(key_list[3], (D, D), D ** -0.5, 0.1875),
        "w_qkv_t": draw_w_qkv_t(jax.random.fold_in(key_list[6], 71), part),
        "w_out_t": normal_values(key_list[5], (D, D), D ** -0.5, 0.1875),
    }


def to_half(values):
    return lax.optimization_barrier(values.astype(jnp.bfloat16))

def layer_norm(values):
    mean = lax.optimization_barrier(jnp.mean(values, axis=-1, keepdims=True))
    centered = values - mean
    var = lax.optimization_barrier(jnp.mean(centered * centered, axis=-1, keepdims=True))
    return centered * lax.rsqrt(var + 1e-06)

def project_in(tokens, shift, scale, w_qkv):
    modulated = (layer_norm(tokens.astype(jnp.float32)) * (1.0 + scale) + shift).astype(jnp.bfloat16)
    qkv = jnp.dot(modulated, w_qkv, preferred_element_type=jnp.float32).astype(jnp.bfloat16)
    return (qkv[..., :D], qkv[..., D:2 * D], qkv[..., 2 * D:])

def attend_rows(query, key, value):
    lead = query.shape[:-1]
    qh = query.reshape(lead + (H, D // H)).astype(jnp.float32)
    kh = key.reshape(lead + (H, D // H)).astype(jnp.float32)
    vh = value.reshape(lead + (H, D // H)).astype(jnp.float32)
    scores = jnp.einsum('lhe,mhe->hlm', qh, kh) / jnp.sqrt(jnp.float32(D // H))
    weights = to_half(jax.nn.softmax(scores, axis=-1)).astype(jnp.float32)
    attended = jnp.einsum('hlm,mhe->lhe', weights, vh)
    return attended.reshape(lead + (D,)).astype(jnp.bfloat16)

def reference(clip, modulation, w_qkv_s, w_out_s, w_qkv_t, w_out_t):
    query, key, value = project_in(clip, modulation[0], modulation[1], w_qkv_s)
    attended = lax.map(lambda trio: attend_rows(trio[0], trio[1], trio[2]), (query, key, value))
    proj = jnp.dot(attended, w_out_s, preferred_element_type=jnp.float32)
    spatial = (clip.astype(jnp.float32) + modulation[2] * proj).astype(jnp.bfloat16)
    query, key, value = project_in(spatial, modulation[3], modulation[4], w_qkv_t)
    swap_q = jnp.swapaxes(query, 0, 1)
    swap_k = jnp.swapaxes(key, 0, 1)
    swap_v = jnp.swapaxes(value, 0, 1)
    attended = lax.map(lambda trio: attend_rows(trio[0], trio[1], trio[2]), (swap_q, swap_k, swap_v))
    attended = jnp.swapaxes(attended, 0, 1)
    proj = jnp.dot(attended, w_out_t, preferred_element_type=jnp.float32)
    return (spatial.astype(jnp.float32) + modulation[5] * proj).astype(jnp.bfloat16)
```

```python
import jax
import jax.numpy as jnp
from jax import lax
from jax.experimental import pallas as pl
from jax.experimental.pallas import tpu as pltpu
from jax.sharding import PartitionSpec as P

D = 1152
H = 16
E = D // H
P_SIZE = 512
SEQ = 32
WIN = 256
CH = 384
NQ = 3 * D // CH
ROWS = P_SIZE
LOG2E = 1.4426950408889634
QSCALE = LOG2E / (E ** 0.5)
VMEM_LIMIT = 56 * 1024 * 1024


def window(h):
    start = min(h * E // 128 * 128, D - WIN)
    return start, h * E - start


def modulate(src, dst, shift, gain, rows, step):
    def block(i, carry):
        r = pl.multiple_of(i * step, step)
        x = src[pl.ds(r, step), :].astype(jnp.float32)
        mean = jnp.sum(x, axis=-1, keepdims=True) * (1.0 / D)
        centered = x - mean
        var = jnp.sum(centered * centered, axis=-1, keepdims=True) * (1.0 / D)
        normed = centered * lax.rsqrt(var + 1e-06)
        dst[pl.ds(r, step), :] = (normed * gain + shift).astype(jnp.bfloat16)
        return carry

    lax.fori_loop(0, rows // step, block, 0, unroll=2)


def weight_copies(w_qkv, w_out, wq, wo, sems):
    copies = [
        pltpu.make_async_copy(
            w_qkv.at[:, pl.ds(j * CH, CH)], wq.at[:, pl.ds(j * CH, CH)], sems.at[j]
        )
        for j in range(NQ)
    ]
    copies.append(pltpu.make_async_copy(w_out, wo, sems.at[NQ]))
    return copies


def project(mod, wq, qkv, copies):
    for j in range(NQ):
        copies[j].wait()
        part = jnp.dot(
            mod[...], wq[:, j * CH : (j + 1) * CH], preferred_element_type=jnp.float32
        )
        if j * CH < D:
            part = part * QSCALE
        qkv[:, j * CH : (j + 1) * CH] = part.astype(jnp.bfloat16)


def finish(x, att, wo, gate, out, rows):
    for j in range(D // CH):
        cols = slice(j * CH, (j + 1) * CH)
        proj = jnp.dot(att[...], wo[:, cols], preferred_element_type=jnp.float32)
        out[:, cols] = (x[:, cols].astype(jnp.float32) + gate[:, cols] * proj).astype(
            jnp.bfloat16
        )


def head_mask(h, rows):
    start, off = window(h)
    lane = lax.broadcasted_iota(jnp.int32, (rows, WIN), 1)
    return (lane >= off) & (lane < off + E)


def attend(q, k, v, h, keep=None):
    mask = head_mask(h, q.shape[0])
    q = jnp.where(mask, q, jnp.zeros_like(q))
    s = lax.dot_general(q, k, (((1,), (1,)), ((), ())), preferred_element_type=jnp.float32)
    if keep is not None:
        s = jnp.where(keep, s, -jnp.inf)
    p = jnp.exp2(s - jnp.max(s, axis=-1, keepdims=True))
    total = jnp.sum(p, axis=-1, keepdims=True)
    o = jnp.dot(p.astype(jnp.bfloat16), v, preferred_element_type=jnp.float32)
    return mask, (o * (1.0 / total)).astype(jnp.bfloat16)


def spatial_kernel(x, modulation, w_qkv, w_out, out, wq, wo, mod, qkv, att, sems):
    copies = weight_copies(w_qkv, w_out, wq, wo, sems)
    for copy in copies:
        copy.start()
    x = x.at[0]
    modulate(x, mod, modulation[0:1, :], 1.0 + modulation[1:2, :], ROWS, 32)
    project(mod, wq, qkv, copies)
    step = 256
    for h in range(H):
        start, _ = window(h)
        k = qkv[:, D + start : D + start + WIN]
        v = qkv[:, 2 * D + start : 2 * D + start + WIN]
        for r in range(0, ROWS, step):
            rows = slice(r, r + step)
            q = qkv[rows, start : start + WIN]
            mask, o = attend(q, k, v, h)
            att[rows, start : start + WIN] = jnp.where(mask, o, att[rows, start : start + WIN])
    copies[NQ].wait()
    finish(x, att, wo, modulation[2:3, :], out, ROWS)


def weight_scratch():
    return [pltpu.VMEM((D, 3 * D), jnp.bfloat16), pltpu.VMEM((D, D), jnp.bfloat16)]


def spatial(clip, modulation, w_qkv, w_out, frame):
    any_spec = pl.BlockSpec(memory_space=pl.ANY)
    return pl.pallas_call(
        spatial_kernel,
        grid=(1,),
        out_shape=jax.ShapeDtypeStruct((ROWS, D), jnp.bfloat16),
        in_specs=[
            pl.BlockSpec((1, ROWS, D), lambda i: (frame, 0, 0)),
            pl.BlockSpec((6, D), lambda i: (0, 0)),
            any_spec,
            any_spec,
        ],
        out_specs=pl.BlockSpec((ROWS, D), lambda i: (0, 0)),
        scratch_shapes=weight_scratch()
        + [
            pltpu.VMEM((ROWS, D), jnp.bfloat16),
            pltpu.VMEM((ROWS, 3 * D), jnp.bfloat16),
            pltpu.VMEM((ROWS, D), jnp.bfloat16),
            pltpu.SemaphoreType.DMA((NQ + 1,)),
        ],
        compiler_params=pltpu.CompilerParams(vmem_limit_bytes=VMEM_LIMIT),
        cost_estimate=pl.CostEstimate(
            flops=9 * 10**9, bytes_accessed=13 * 10**6, transcendentals=4 * 10**6
        ),
        name="spatial",
    )(clip, modulation, w_qkv, w_out)


PATCHES = P_SIZE // SEQ
FRAMES = 2 * SEQ
TOKENS = FRAMES * PATCHES
BLOCK = 16 * PATCHES
GROUPS = TOKENS // BLOCK


def permutation(dtype):
    row = lax.broadcasted_iota(jnp.int32, (BLOCK, BLOCK), 0)
    col = lax.broadcasted_iota(jnp.int32, (BLOCK, BLOCK), 1)
    return (((row & 15) == (col >> 4)) & ((row >> 4) == (col & 15))).astype(dtype)


def temporal_kernel(
    x0, x1, modulation, w_qkv, w_out, out, wq, wo, toks, mod, qkv, att, res, sems
):
    copies = weight_copies(w_qkv, w_out, wq, wo, sems)
    for copy in copies:
        copy.start()
    swap = permutation(jnp.bfloat16)
    for g in range(GROUPS):
        src = (x0, x1)[g // 2]
        rows = src[(g % 2) * BLOCK : (g % 2 + 1) * BLOCK, :]
        moved = jnp.dot(swap, rows, preferred_element_type=jnp.float32).astype(jnp.bfloat16)
        for p in range(PATCHES):
            at = p * FRAMES + g * 16
            toks[at : at + 16, :] = moved[p * 16 : (p + 1) * 16, :]
    modulate(toks, mod, modulation[3:4, :], 1.0 + modulation[4:5, :], TOKENS, 32)
    project(mod, wq, qkv, copies)
    pair = 2 * FRAMES
    keep = (lax.broadcasted_iota(jnp.int32, (pair, pair), 0) // FRAMES) == (
        lax.broadcasted_iota(jnp.int32, (pair, pair), 1) // FRAMES
    )

    def one_pair(i, carry):
        rows = pl.ds(pl.multiple_of(i * pair, pair), pair)
        for h in range(H):
            start, _ = window(h)
            q = qkv[rows, start : start + WIN]
            k = qkv[rows, D + start : D + start + WIN]
            v = qkv[rows, 2 * D + start : 2 * D + start + WIN]
            mask, o = attend(q, k, v, h, keep)
            att[rows, start : start + WIN] = jnp.where(mask, o, att[rows, start : start + WIN])
        return carry

    lax.fori_loop(0, TOKENS // pair, one_pair, 0)
    copies[NQ].wait()
    finish(toks, att, wo, modulation[5:6, :], res, TOKENS)
    for g in range(GROUPS):
        rows = jnp.concatenate(
            [res[p * FRAMES + g * 16 : p * FRAMES + g * 16 + 16, :] for p in range(PATCHES)], axis=0
        )
        moved = jnp.dot(swap, rows, preferred_element_type=jnp.float32).astype(jnp.bfloat16)
        f = g // 2
        base = (g % 2) * 16
        out[base : base + 16, f] = moved.reshape(16, PATCHES, D)


def temporal(x0, x1, modulation, w_qkv, w_out):
    any_spec = pl.BlockSpec(memory_space=pl.ANY)
    return pl.pallas_call(
        temporal_kernel,
        grid=(1,),
        out_shape=jax.ShapeDtypeStruct((SEQ, 2, PATCHES, D), jnp.bfloat16),
        in_specs=[
            pl.BlockSpec((ROWS, D), lambda i: (0, 0)),
            pl.BlockSpec((ROWS, D), lambda i: (0, 0)),
            pl.BlockSpec((6, D), lambda i: (0, 0)),
            any_spec,
            any_spec,
        ],
        out_specs=pl.BlockSpec((SEQ, 2, PATCHES, D), lambda i: (0, 0, 0, 0)),
        scratch_shapes=weight_scratch()
        + [
            pltpu.VMEM((TOKENS, D), jnp.bfloat16),
            pltpu.VMEM((TOKENS, D), jnp.bfloat16),
            pltpu.VMEM((TOKENS, 3 * D), jnp.bfloat16),
            pltpu.VMEM((TOKENS, D), jnp.bfloat16),
            pltpu.VMEM((TOKENS, D), jnp.bfloat16),
            pltpu.SemaphoreType.DMA((NQ + 1,)),
        ],
        compiler_params=pltpu.CompilerParams(vmem_limit_bytes=VMEM_LIMIT),
        cost_estimate=pl.CostEstimate(
            flops=13 * 10**9, bytes_accessed=15 * 10**6, transcendentals=2 * 10**6
        ),
        name="temporal",
    )(x0, x1, modulation, w_qkv, w_out)


def exchange(x):
    return lax.all_to_all(x, "seq", split_axis=0, concat_axis=0, tiled=True)


def body(clip, modulation, w_qkv_s, w_out_s, w_qkv_t, w_out_t):
    got = []
    for frame in range(2):
        sent = spatial(clip, modulation, w_qkv_s, w_out_s, frame)
        got.append(exchange(sent.reshape(SEQ, PATCHES, D)).reshape(ROWS, D))
    result = temporal(got[0], got[1], modulation, w_qkv_t, w_out_t)
    back = exchange(result)
    return jnp.swapaxes(back, 0, 1).reshape(2, P_SIZE, D)


def solution(mesh):
    return jax.shard_map(
        body,
        mesh=mesh,
        in_specs=(P(("dp", "seq"), None, None), P("dp", None), P(), P(), P(), P()),
        out_specs=P(("dp", "seq"), None, None),
        check_vma=False,
    )
```

```python
import jax
import jax.numpy as jnp
from jax import lax
from jax.experimental import pallas as pl
from jax.experimental.pallas import tpu as pltpu
from jax.sharding import PartitionSpec as P

D = 1152
H = 16
E = D // H
P_SIZE = 512
SEQ = 32
WIN = 256
ROWS = P_SIZE
PATCHES = P_SIZE // SEQ
PAIRS = PATCHES // 2
PAIR = 2 * 2 * SEQ
QUARTER = PAIR // 4
BLOCK = 16 * PATCHES
QSCALE = 1.4426950408889634 / (E ** 0.5)
MIB = 1024 * 1024
STEP = 256


def pieces(width, size):
    return [(c, min(size, width - c)) for c in range(0, width, size)]


QKV_PIECES = pieces(3 * D, 512)
OUT_PIECES = pieces(D, 512)


def modulate(src, dst, shift, gain, rows, step=32):
    for r in range(rows.start, rows.stop, step):
        x = src[r : r + step, :].astype(jnp.float32)
        mean = jnp.sum(x, axis=-1, keepdims=True) * (1.0 / D)
        centered = x - mean
        var = jnp.sum(centered * centered, axis=-1, keepdims=True) * (1.0 / D)
        normed = centered * lax.rsqrt(var + 1e-06)
        dst[r : r + step, :] = (normed * gain + shift).astype(jnp.bfloat16)


def project(mod, wq, piece):
    c, n = piece
    part = jnp.dot(mod, wq[:, c : c + n], preferred_element_type=jnp.float32)
    if c + n <= D:
        part = part * QSCALE
    elif c < D:
        lane = lax.broadcasted_iota(jnp.int32, (1, n), 1)
        part = part * jnp.where(lane < D - c, QSCALE, 1.0)
    return part.astype(jnp.bfloat16)


def finish(x, att, wo, gate, res, rows):
    for c, n in OUT_PIECES:
        cols = slice(c, c + n)
        proj = jnp.dot(att, wo[:, cols], preferred_element_type=jnp.float32)
        res[rows, cols] = (x[rows, cols].astype(jnp.float32) + gate[:, cols] * proj).astype(
            jnp.bfloat16
        )


def attend(load, store, keep=None):
    lane = lax.broadcasted_iota(jnp.int32, (1, WIN), 1)
    columns = {}
    for h in range(H):
        start = min(h * E // 128 * 128, D - WIN)
        off = h * E - start
        mine = ((lane >= off) & (lane < off + E)).astype(jnp.float32).astype(jnp.bfloat16)
        q = load(0, start) * mine
        s = lax.dot_general(
            q, load(1, start), (((1,), (1,)), ((), ())), preferred_element_type=jnp.float32
        )
        if keep is not None:
            s = jnp.where(keep, s, -jnp.inf)
        p = jnp.exp2(s - jnp.max(s, axis=-1, keepdims=True))
        total = jnp.sum(p, axis=-1, keepdims=True)
        o = jnp.dot(p.astype(jnp.bfloat16), load(2, start), preferred_element_type=jnp.float32)
        o = o * (1.0 / total)
        for side in (0, 1):
            c = start + side * 128
            low, high = max(h * E - c, 0), min(h * E + E - c, 128)
            if low >= high:
                continue
            part = o[:, side * 128 : side * 128 + 128]
            if low > 0:
                part = jnp.where(lane[:, :128] >= low, part, columns[c])
            columns[c] = part
            if high == 128:
                store(c, part.astype(jnp.bfloat16))


class Loads:
    def __init__(self, sems):
        self.sems = sems
        self.copies = []

    def start(self, source, target):
        copy = pltpu.make_async_copy(source, target, self.sems.at[len(self.copies)])
        copy.start()
        self.copies.append(copy)
        return copy


def start_tokens(loads, source, target):
    return [
        loads.start(source.at[pl.ds(r, STEP), :], target.at[pl.ds(r, STEP), :])
        for r in range(0, ROWS, STEP)
    ]


def start_qkv_weights(loads, w_qkv, wq):
    return [
        loads.start(w_qkv.at[:, pl.ds(c, n)], wq.at[:, pl.ds(c, n)]) for c, n in QKV_PIECES
    ]


def project_rows(norm, tokens, weights, product):
    ahead = 2
    tokens[0].wait()
    norm(0)
    tokens[1].wait()
    for j in range(ahead):
        weights[j].wait()
    for j in range(ahead):
        product(0, j)
    norm(STEP)
    for j in range(ahead):
        product(STEP, j)
    for j in range(ahead, len(QKV_PIECES)):
        weights[j].wait()
        for r in (0, STEP):
            product(r, j)


def spatial_kernel(
    frame, clip, modulation, w_qkv, w_out, out, rows6, x, wq, wo, mod, qkv, att, res, sems, sent
):
    loads = Loads(sems)
    first = loads.start(modulation, rows6)
    tokens = start_tokens(loads, clip.at[frame], x)
    weights = start_qkv_weights(loads, w_qkv, wq)
    last = loads.start(w_out, wo)
    first.wait()
    shift, gain, gate = rows6[0:1, :], 1.0 + rows6[1:2, :], rows6[2:3, :]

    def norm(r):
        modulate(x, mod, shift, gain, slice(r, r + STEP))

    def product(r, j):
        c, n = QKV_PIECES[j]
        qkv[r : r + STEP, c : c + n] = project(mod[r : r + STEP, :], wq, (c, n))

    project_rows(norm, tokens, weights, product)
    last.wait()
    done = []
    for i, r in enumerate(range(0, ROWS, STEP)):

        def load(which, c):
            rows = slice(r, r + STEP) if which == 0 else slice(0, ROWS)
            return qkv[rows, which * D + c : which * D + c + WIN]

        def store(c, part):
            att[r : r + STEP, c : c + 128] = part

        attend(load, store)
        finish(x, att[r : r + STEP, :], wo, gate, res, slice(r, r + STEP))
        done.append(
            pltpu.make_async_copy(
                res.at[pl.ds(r, STEP), :], out.at[pl.ds(r, STEP), :], sent.at[i]
            )
        )
        done[-1].start()
    for copy in done:
        copy.wait()


def call(kernel, name, out_shape, operands, scratch, copies_in, copies_out, flops, exps):
    anywhere = pl.BlockSpec(memory_space=pl.ANY)
    return pl.pallas_call(
        kernel,
        out_shape=out_shape,
        in_specs=[anywhere] * len(operands),
        out_specs=anywhere,
        scratch_shapes=scratch
        + [pltpu.SemaphoreType.DMA((copies_in,)), pltpu.SemaphoreType.DMA((copies_out,))],
        compiler_params=pltpu.CompilerParams(vmem_limit_bytes=60 * MIB),
        cost_estimate=pl.CostEstimate(
            flops=flops, bytes_accessed=15 * 10**6, transcendentals=exps
        ),
        name=name,
    )(*operands)


def buffer(*shape):
    return pltpu.VMEM(shape, jnp.bfloat16)


def spatial(clip, modulation, w_qkv, w_out, frame):
    def kernel(*refs):
        spatial_kernel(frame, *refs)

    return call(
        kernel,
        "spatial%d" % frame,
        jax.ShapeDtypeStruct((ROWS, D), jnp.bfloat16),
        (clip, modulation, w_qkv, w_out),
        [
            pltpu.VMEM((6, D), jnp.float32),
            buffer(ROWS, D),
            buffer(D, 3 * D),
            buffer(D, D),
            buffer(ROWS, D),
            buffer(ROWS, 3 * D),
            buffer(ROWS, D),
            buffer(ROWS, D),
        ],
        1 + ROWS // STEP + len(QKV_PIECES) + 1,
        ROWS // STEP,
        8 * 10**9,
        4 * 10**6,
    )


def permutation():
    row = lax.broadcasted_iota(jnp.int32, (BLOCK, BLOCK), 0)
    col = lax.broadcasted_iota(jnp.int32, (BLOCK, BLOCK), 1)
    swap = ((row & 15) == (col >> 4)) & ((row >> 4) == (col & 15))
    return swap.astype(jnp.float32).astype(jnp.bfloat16)


def move(swap, rows):
    return jnp.dot(swap, rows, preferred_element_type=jnp.float32).astype(jnp.bfloat16)


def temporal_project(x, mod, moved, wq, swap, shift, gain, tokens, weights, put):
    def norm(r):
        modulate(x, mod, shift, gain, slice(r, r + STEP))
        moved[r : r + STEP, :] = move(swap, mod[r : r + STEP, :])

    def product(r, j):
        c, n = QKV_PIECES[j]
        put(r // STEP, c, n, project(moved[r : r + STEP, :], wq, (c, n)))

    project_rows(norm, tokens, weights, product)


def temporal_in_kernel(
    tokens0, modulation, w_qkv, qkv_out, rows6, x, wq, mod, moved, qkv, sems, sent
):
    loads = Loads(sems)
    first = loads.start(modulation, rows6)
    tokens = start_tokens(loads, tokens0, x)
    weights = start_qkv_weights(loads, w_qkv, wq)
    first.wait()
    done = []

    def put(g, c, n, part):
        qkv[:, g * QUARTER : (g + 1) * QUARTER, c : c + n] = part.reshape(PAIRS, QUARTER, n)
        if g == 1:
            done.append(
                pltpu.make_async_copy(
                    qkv.at[:, :, pl.ds(c, n)], qkv_out.at[:, :, pl.ds(c, n)], sent.at[len(done)]
                )
            )
            done[-1].start()

    temporal_project(
        x, mod, moved, wq, permutation(), rows6[3:4, :], 1.0 + rows6[4:5, :], tokens, weights, put
    )
    for copy in done:
        copy.wait()


def temporal_in(tokens0, modulation, w_qkv):
    return call(
        temporal_in_kernel,
        "temporal_in",
        jax.ShapeDtypeStruct((PAIRS, 2 * QUARTER, 3 * D), jnp.bfloat16),
        (tokens0, modulation, w_qkv),
        [
            pltpu.VMEM((6, D), jnp.float32),
            buffer(ROWS, D),
            buffer(D, 3 * D),
            buffer(ROWS, D),
            buffer(ROWS, D),
            buffer(PAIRS, 2 * QUARTER, 3 * D),
        ],
        1 + ROWS // STEP + len(QKV_PIECES),
        len(QKV_PIECES),
        5 * 10**9,
        1000,
    )


def temporal_out_kernel(
    tokens1, tokens0, qkv0, modulation, w_qkv, w_out, out,
    rows6, x1, x0, wq, wo, mod, moved, qkv, att, res, sems, sent,
):
    loads = Loads(sems)
    first = loads.start(modulation, rows6)
    tokens = start_tokens(loads, tokens1, x1)
    weights = start_qkv_weights(loads, w_qkv, wq)
    early = loads.start(qkv0, qkv.at[:, pl.ds(0, 2 * QUARTER), :])
    last = [loads.start(w_out, wo), loads.start(tokens0, x0)]
    first.wait()
    swap = permutation()

    def put(g, c, n, part):
        at = (2 + g) * QUARTER
        qkv[:, at : at + QUARTER, c : c + n] = part.reshape(PAIRS, QUARTER, n)

    temporal_project(
        x1, mod, moved, wq, swap, rows6[3:4, :], 1.0 + rows6[4:5, :], tokens, weights, put
    )
    early.wait()
    keep = (lax.broadcasted_iota(jnp.int32, (PAIR, PAIR), 0) // 16 % 2) == (
        lax.broadcasted_iota(jnp.int32, (PAIR, PAIR), 1) // 16 % 2
    )

    def one_pair(i, carry):
        def load(which, c):
            return qkv[i, :, which * D + c : which * D + c + WIN]

        def store(c, part):
            rows = pl.ds(pl.multiple_of(i * QUARTER, QUARTER), QUARTER)
            for k in range(4):
                att[k, rows, c : c + 128] = part[k * QUARTER : (k + 1) * QUARTER]

        attend(load, store, keep)
        return carry

    lax.fori_loop(0, PAIRS, one_pair, 0, unroll=2)
    for copy in last:
        copy.wait()
    done = []
    for k in range(4):
        f, g = k // 2, k % 2
        back = move(swap, att[k])
        rows = slice(g * BLOCK, (g + 1) * BLOCK)
        finish((x0, x1)[f], back, wo, rows6[5:6, :], res.at[f], rows)
        for a in range(16):
            done.append(
                pltpu.make_async_copy(
                    res.at[f, pl.ds(g * BLOCK + a * 16, 16), :], out.at[g * 16 + a, f], sent.at[k * 16 + a]
                )
            )
            done[-1].start()
    for copy in done:
        copy.wait()


def temporal_out(tokens1, tokens0, qkv0, modulation, w_qkv, w_out):
    return call(
        temporal_out_kernel,
        "temporal_out",
        jax.ShapeDtypeStruct((SEQ, 2, PATCHES, D), jnp.bfloat16),
        (tokens1, tokens0, qkv0, modulation, w_qkv, w_out),
        [
            pltpu.VMEM((6, D), jnp.float32),
            buffer(ROWS, D),
            buffer(ROWS, D),
            buffer(D, 3 * D),
            buffer(D, D),
            buffer(ROWS, D),
            buffer(ROWS, D),
            buffer(PAIRS, PAIR, 3 * D),
            buffer(4, BLOCK, D),
            buffer(2, ROWS, D),
        ],
        1 + ROWS // STEP + len(QKV_PIECES) + 3,
        64,
        8 * 10**9,
        2 * 10**6,
    )


def exchange(x):
    return lax.all_to_all(x, "seq", split_axis=0, concat_axis=0, tiled=True)


def body(clip, modulation, w_qkv_s, w_out_s, w_qkv_t, w_out_t):
    got = []
    for frame in range(2):
        sent = spatial(clip, modulation, w_qkv_s, w_out_s, frame)
        got.append(exchange(sent.reshape(SEQ, PATCHES, D)).reshape(ROWS, D))
    qkv0 = temporal_in(got[0], modulation, w_qkv_t)
    result = temporal_out(got[1], got[0], qkv0, modulation, w_qkv_t, w_out_t)
    back = exchange(result)
    return jnp.swapaxes(back, 0, 1).reshape(2, P_SIZE, D)


def solution(mesh):
    return jax.shard_map(
        body,
        mesh=mesh,
        in_specs=(P(("dp", "seq"), None, None), P("dp", None), P(), P(), P(), P()),
        out_specs=P(("dp", "seq"), None, None),
        check_vma=False,
    )
```

```python
import jax
import jax.numpy as jnp
from jax import lax
from jax.experimental import pallas as pl
from jax.experimental.pallas import tpu as pltpu
from jax.sharding import PartitionSpec as P

D = 1152
H = 16
E = D // H
P_SIZE = 512
SEQ = 32
WIN = 256
ROWS = P_SIZE
PATCHES = P_SIZE // SEQ
PAIRS = PATCHES // 2
PAIR = 2 * 2 * SEQ
QUARTER = PAIR // 4
BLOCK = 16 * PATCHES
QSCALE = 1.4426950408889634 / (E ** 0.5)
MIB = 1024 * 1024
STEP = 256
DEPTH = 6
VMEM_BYTES = 64 * MIB - 256 * 1024


def pieces(width, size):
    return [(c, min(size, width - c)) for c in range(0, width, size)]


QKV_PIECES = pieces(3 * D, 512)
OUT_PIECES = pieces(D, 512)


def modulate(src, dst, shift, gain, rows, step=32):
    for r in range(rows.start, rows.stop, step):
        x = src[r : r + step, :].astype(jnp.float32)
        mean = jnp.sum(x, axis=-1, keepdims=True) * (1.0 / D)
        centered = x - mean
        var = jnp.sum(centered * centered, axis=-1, keepdims=True) * (1.0 / D)
        normed = centered * lax.rsqrt(var + 1e-06)
        dst[r : r + step, :] = (normed * gain + shift).astype(jnp.bfloat16)


def project(mod, wq, piece):
    c, n = piece
    part = jnp.dot(mod, wq[:, c : c + n], preferred_element_type=jnp.float32)
    if c + n <= D:
        part = part * QSCALE
    elif c < D:
        lane = lax.broadcasted_iota(jnp.int32, (1, n), 1)
        part = part * jnp.where(lane < D - c, QSCALE, 1.0)
    return part.astype(jnp.bfloat16)


def finish(x, att, wo, gate, res, rows):
    for c, n in OUT_PIECES:
        cols = slice(c, c + n)
        proj = jnp.dot(att, wo[:, cols], preferred_element_type=jnp.float32)
        res[rows, cols] = (x[rows, cols].astype(jnp.float32) + gate[:, cols] * proj).astype(
            jnp.bfloat16
        )


def attend(load, store, keep=None):
    lane = lax.broadcasted_iota(jnp.int32, (1, WIN), 1)
    columns = {}
    for h in range(H):
        start = min(h * E // 128 * 128, D - WIN)
        off = h * E - start
        mine = ((lane >= off) & (lane < off + E)).astype(jnp.float32).astype(jnp.bfloat16)
        q = load(0, start) * mine
        s = lax.dot_general(
            q, load(1, start), (((1,), (1,)), ((), ())), preferred_element_type=jnp.float32
        )
        if keep is not None:
            s = jnp.where(keep, s, -jnp.inf)
        p = jnp.exp2(s - jnp.max(s, axis=-1, keepdims=True))
        total = jnp.sum(p, axis=-1, keepdims=True)
        o = jnp.dot(p.astype(jnp.bfloat16), load(2, start), preferred_element_type=jnp.float32)
        o = o * (1.0 / total)
        for side in (0, 1):
            c = start + side * 128
            low, high = max(h * E - c, 0), min(h * E + E - c, 128)
            if low >= high:
                continue
            part = o[:, side * 128 : side * 128 + 128]
            if low > 0:
                part = jnp.where(lane[:, :128] >= low, part, columns[c])
            columns[c] = part
            if high == 128:
                store(c, part.astype(jnp.bfloat16))


class Loads:
    def __init__(self, sems):
        self.sems = sems
        self.copies = []
        self.started = 0

    def add(self, source, target):
        at = len(self.copies)
        self.copies.append(pltpu.make_async_copy(source, target, self.sems.at[at]))
        return at

    def start(self, count=1):
        for copy in self.copies[self.started : self.started + count]:
            copy.start()
        self.started += count

    def wait(self, at):
        self.copies[at].wait()
        self.start()


def add_tokens(loads, source, target):
    return [
        loads.add(source.at[pl.ds(r, STEP), :], target.at[pl.ds(r, STEP), :])
        for r in range(0, ROWS, STEP)
    ]


def add_qkv_weights(loads, w_qkv, wq):
    return [
        loads.add(w_qkv.at[:, pl.ds(c, n)], wq.at[:, pl.ds(c, n)]) for c, n in QKV_PIECES
    ]


def project_rows(norm, loads, tokens, weights, product):
    ahead = 2
    loads.wait(tokens[0])
    norm(0)
    loads.wait(tokens[1])
    for j in range(ahead):
        loads.wait(weights[j])
    for j in range(ahead):
        product(0, j)
    norm(STEP)
    for j in range(ahead):
        product(STEP, j)
    for j in range(ahead, len(QKV_PIECES)):
        loads.wait(weights[j])
        for r in (0, STEP):
            product(r, j)


def spatial_kernel(
    frame, clip, modulation, w_qkv, w_out, out, rows6, x, wq, wo, mod, qkv, att, res, sems, sent
):
    loads = Loads(sems)
    first = loads.add(modulation, rows6)
    tokens = add_tokens(loads, clip.at[frame], x)
    weights = add_qkv_weights(loads, w_qkv, wq)
    last = loads.add(w_out, wo)
    loads.start(DEPTH)
    loads.wait(first)
    shift, gain, gate = rows6[0:1, :], 1.0 + rows6[1:2, :], rows6[2:3, :]

    def norm(r):
        modulate(x, mod, shift, gain, slice(r, r + STEP))

    def product(r, j):
        c, n = QKV_PIECES[j]
        qkv[r : r + STEP, c : c + n] = project(mod[r : r + STEP, :], wq, (c, n))

    project_rows(norm, loads, tokens, weights, product)
    loads.wait(last)
    done = []
    for i, r in enumerate(range(0, ROWS, STEP)):

        def load(which, c):
            rows = slice(r, r + STEP) if which == 0 else slice(0, ROWS)
            return qkv[rows, which * D + c : which * D + c + WIN]

        def store(c, part):
            att[r : r + STEP, c : c + 128] = part

        attend(load, store)
        finish(x, att[r : r + STEP, :], wo, gate, res, slice(r, r + STEP))
        done.append(
            pltpu.make_async_copy(
                res.at[pl.ds(r, STEP), :], out.at[pl.ds(r, STEP), :], sent.at[i]
            )
        )
        done[-1].start()
    for copy in done:
        copy.wait()


def call(kernel, name, out_shape, operands, scratch, copies_in, copies_out, flops, exps):
    anywhere = pl.BlockSpec(memory_space=pl.ANY)
    return pl.pallas_call(
        kernel,
        out_shape=out_shape,
        in_specs=[anywhere] * len(operands),
        out_specs=anywhere,
        scratch_shapes=scratch
        + [pltpu.SemaphoreType.DMA((copies_in,)), pltpu.SemaphoreType.DMA((copies_out,))],
        compiler_params=pltpu.CompilerParams(vmem_limit_bytes=VMEM_BYTES),
        cost_estimate=pl.CostEstimate(
            flops=flops, bytes_accessed=15 * 10**6, transcendentals=exps
        ),
        name=name,
    )(*operands)


def buffer(*shape):
    return pltpu.VMEM(shape, jnp.bfloat16)


def spatial(clip, modulation, w_qkv, w_out, frame):
    def kernel(*refs):
        spatial_kernel(frame, *refs)

    return call(
        kernel,
        "spatial%d" % frame,
        jax.ShapeDtypeStruct((ROWS, D), jnp.bfloat16),
        (clip, modulation, w_qkv, w_out),
        [
            pltpu.VMEM((6, D), jnp.float32),
            buffer(ROWS, D),
            buffer(D, 3 * D),
            buffer(D, D),
            buffer(ROWS, D),
            buffer(ROWS, 3 * D),
            buffer(ROWS, D),
            buffer(ROWS, D),
        ],
        1 + ROWS // STEP + len(QKV_PIECES) + 1,
        ROWS // STEP,
        8 * 10**9,
        4 * 10**6,
    )


def permutation():
    row = lax.broadcasted_iota(jnp.int32, (BLOCK, BLOCK), 0)
    col = lax.broadcasted_iota(jnp.int32, (BLOCK, BLOCK), 1)
    swap = ((row & 15) == (col >> 4)) & ((row >> 4) == (col & 15))
    return swap.astype(jnp.float32).astype(jnp.bfloat16)


def move(swap, rows):
    return jnp.dot(swap, rows, preferred_element_type=jnp.float32).astype(jnp.bfloat16)


def temporal_project(x, mod, moved, wq, swap, shift, gain, loads, tokens, weights, put):
    def norm(r):
        modulate(x, mod, shift, gain, slice(r, r + STEP))
        moved[r : r + STEP, :] = move(swap, mod[r : r + STEP, :])

    def product(r, j):
        c, n = QKV_PIECES[j]
        put(r // STEP, c, n, project(moved[r : r + STEP, :], wq, (c, n)))

    project_rows(norm, loads, tokens, weights, product)


def temporal_in_kernel(
    tokens0, modulation, w_qkv, qkv_out, rows6, x, wq, mod, moved, qkv, sems, sent
):
    loads = Loads(sems)
    first = loads.add(modulation, rows6)
    tokens = add_tokens(loads, tokens0, x)
    weights = add_qkv_weights(loads, w_qkv, wq)
    loads.start(DEPTH)
    loads.wait(first)
    done = []

    def put(g, c, n, part):
        qkv[:, g * QUARTER : (g + 1) * QUARTER, c : c + n] = part.reshape(PAIRS, QUARTER, n)
        if g == 1:
            done.append(
                pltpu.make_async_copy(
                    qkv.at[:, :, pl.ds(c, n)], qkv_out.at[:, :, pl.ds(c, n)], sent.at[len(done)]
                )
            )
            done[-1].start()

    temporal_project(
        x, mod, moved, wq, permutation(), rows6[3:4, :], 1.0 + rows6[4:5, :], loads, tokens, weights, put
    )
    for copy in done:
        copy.wait()


def temporal_in(tokens0, modulation, w_qkv):
    return call(
        temporal_in_kernel,
        "temporal_in",
        jax.ShapeDtypeStruct((PAIRS, 2 * QUARTER, 3 * D), jnp.bfloat16),
        (tokens0, modulation, w_qkv),
        [
            pltpu.VMEM((6, D), jnp.float32),
            buffer(ROWS, D),
            buffer(D, 3 * D),
            buffer(ROWS, D),
            buffer(ROWS, D),
            buffer(PAIRS, 2 * QUARTER, 3 * D),
        ],
        1 + ROWS // STEP + len(QKV_PIECES),
        len(QKV_PIECES),
        5 * 10**9,
        1000,
    )


def temporal_out_kernel(
    tokens1, tokens0, qkv0, modulation, w_qkv, w_out, out,
    rows6, x1, x0, wq, wo, mod, moved, qkv, att, res, sems, sent,
):
    loads = Loads(sems)
    first = loads.add(modulation, rows6)
    tokens = add_tokens(loads, tokens1, x1)
    weights = add_qkv_weights(loads, w_qkv, wq)
    early = loads.add(qkv0, qkv.at[:, pl.ds(0, 2 * QUARTER), :])
    last = [loads.add(w_out, wo), loads.add(tokens0, x0)]
    loads.start(DEPTH)
    loads.wait(first)
    swap = permutation()

    def put(g, c, n, part):
        at = (2 + g) * QUARTER
        qkv[:, at : at + QUARTER, c : c + n] = part.reshape(PAIRS, QUARTER, n)

    temporal_project(
        x1, mod, moved, wq, swap, rows6[3:4, :], 1.0 + rows6[4:5, :], loads, tokens, weights, put
    )
    loads.wait(early)
    keep = (lax.broadcasted_iota(jnp.int32, (PAIR, PAIR), 0) // 16 % 2) == (
        lax.broadcasted_iota(jnp.int32, (PAIR, PAIR), 1) // 16 % 2
    )

    def one_pair(i):
        def load(which, c):
            return qkv[i, :, which * D + c : which * D + c + WIN]

        def store(c, part):
            rows = slice(i * QUARTER, (i + 1) * QUARTER)
            for k in range(4):
                att[k, rows, c : c + 128] = part[k * QUARTER : (k + 1) * QUARTER]

        attend(load, store, keep)

    for i in range(PAIRS):
        one_pair(i)
    for at in last:
        loads.wait(at)
    done = []
    for k in range(4):
        f, g = k // 2, k % 2
        back = move(swap, att[k])
        rows = slice(g * BLOCK, (g + 1) * BLOCK)
        finish((x0, x1)[f], back, wo, rows6[5:6, :], res.at[f], rows)
        for a in range(16):
            done.append(
                pltpu.make_async_copy(
                    res.at[f, pl.ds(g * BLOCK + a * 16, 16), :], out.at[g * 16 + a, f], sent.at[k * 16 + a]
                )
            )
            done[-1].start()
    for copy in done:
        copy.wait()


def temporal_out(tokens1, tokens0, qkv0, modulation, w_qkv, w_out):
    return call(
        temporal_out_kernel,
        "temporal_out",
        jax.ShapeDtypeStruct((SEQ, 2, PATCHES, D), jnp.bfloat16),
        (tokens1, tokens0, qkv0, modulation, w_qkv, w_out),
        [
            pltpu.VMEM((6, D), jnp.float32),
            buffer(ROWS, D),
            buffer(ROWS, D),
            buffer(D, 3 * D),
            buffer(D, D),
            buffer(ROWS, D),
            buffer(ROWS, D),
            buffer(PAIRS, PAIR, 3 * D),
            buffer(4, BLOCK, D),
            buffer(2, ROWS, D),
        ],
        1 + ROWS // STEP + len(QKV_PIECES) + 3,
        64,
        8 * 10**9,
        2 * 10**6,
    )


def exchange(x):
    return lax.all_to_all(x, "seq", split_axis=0, concat_axis=0, tiled=True)


def body(clip, modulation, w_qkv_s, w_out_s, w_qkv_t, w_out_t):
    got = []
    for frame in range(2):
        sent = spatial(clip, modulation, w_qkv_s, w_out_s, frame)
        got.append(exchange(sent.reshape(SEQ, PATCHES, D)).reshape(ROWS, D))
    qkv0 = temporal_in(got[0], modulation, w_qkv_t)
    result = temporal_out(got[1], got[0], qkv0, modulation, w_qkv_t, w_out_t)
    back = exchange(result)
    return jnp.swapaxes(back, 0, 1).reshape(2, P_SIZE, D)


def solution(mesh):
    return jax.shard_map(
        body,
        mesh=mesh,
        in_specs=(P(("dp", "seq"), None, None), P("dp", None), P(), P(), P(), P()),
        out_specs=P(("dp", "seq"), None, None),
        check_vma=False,
    )
```

```python
import jax
import jax.numpy as jnp
from jax import lax
from jax.experimental import pallas as pl
from jax.experimental.pallas import tpu as pltpu
from jax.sharding import PartitionSpec as P

D = 1152
H = 16
E = D // H
P_SIZE = 512
SEQ = 32
WIN = 256
ROWS = P_SIZE
PATCHES = P_SIZE // SEQ
PAIRS = PATCHES // 2
PAIR = 2 * 2 * SEQ
QUARTER = PAIR // 4
BLOCK = 16 * PATCHES
QSCALE = 1.4426950408889634 / (E ** 0.5)
MIB = 1024 * 1024
STEP = 256
DEPTH = 6
QKV_GROUPS = ((1, 2), (3, 4), (5, 6))
FRONT = 128
VMEM_BYTES = 64 * MIB - 256 * 1024


def pieces(width, size):
    return [(c, min(size, width - c)) for c in range(0, width, size)]


QKV_PIECES = pieces(3 * D, 512)
OUT_PIECES = pieces(D, 512)


def modulate(src, dst, shift, gain, rows, step=32):
    for r in range(rows.start, rows.stop, step):
        x = src[r : r + step, :].astype(jnp.float32)
        mean = jnp.sum(x, axis=-1, keepdims=True) * (1.0 / D)
        centered = x - mean
        var = jnp.sum(centered * centered, axis=-1, keepdims=True) * (1.0 / D)
        normed = centered * lax.rsqrt(var + 1e-06)
        dst[r : r + step, :] = (normed * gain + shift).astype(jnp.bfloat16)


def project(mod, wq, piece):
    c, n = piece
    part = jnp.dot(mod, wq[:, c : c + n], preferred_element_type=jnp.float32)
    if c + n <= D:
        part = part * QSCALE
    elif c < D:
        lane = lax.broadcasted_iota(jnp.int32, (1, n), 1)
        part = part * jnp.where(lane < D - c, QSCALE, 1.0)
    return part.astype(jnp.bfloat16)


def finish(x, att, wo, gate, res, rows):
    for c, n in OUT_PIECES:
        cols = slice(c, c + n)
        proj = jnp.dot(att, wo[:, cols], preferred_element_type=jnp.float32)
        res[rows, cols] = (x[rows, cols].astype(jnp.float32) + gate[:, cols] * proj).astype(
            jnp.bfloat16
        )


def attend(load, store, keep=None):
    lane = lax.broadcasted_iota(jnp.int32, (1, WIN), 1)
    columns = {}
    for h in range(H):
        start = min(h * E // 128 * 128, D - WIN)
        off = h * E - start
        mine = ((lane >= off) & (lane < off + E)).astype(jnp.float32).astype(jnp.bfloat16)
        q = load(0, start) * mine
        s = lax.dot_general(
            q, load(1, start), (((1,), (1,)), ((), ())), preferred_element_type=jnp.float32
        )
        if keep is not None:
            s = jnp.where(keep, s, -jnp.inf)
        p = jnp.exp2(s - jnp.max(s, axis=-1, keepdims=True))
        total = jnp.sum(p, axis=-1, keepdims=True)
        o = jnp.dot(p.astype(jnp.bfloat16), load(2, start), preferred_element_type=jnp.float32)
        o = o * (1.0 / total)
        for side in (0, 1):
            c = start + side * 128
            low, high = max(h * E - c, 0), min(h * E + E - c, 128)
            if low >= high:
                continue
            part = o[:, side * 128 : side * 128 + 128]
            if low > 0:
                part = jnp.where(lane[:, :128] >= low, part, columns[c])
            columns[c] = part
            if high == 128:
                store(c, part.astype(jnp.bfloat16))


class Loads:
    def __init__(self, sems):
        self.sems = sems
        self.copies = []
        self.started = 0

    def add(self, source, target):
        at = len(self.copies)
        self.copies.append(pltpu.make_async_copy(source, target, self.sems.at[at]))
        return at

    def start(self, count=1):
        for copy in self.copies[self.started : self.started + count]:
            copy.start()
        self.started += count

    def wait(self, at):
        self.copies[at].wait()
        self.start()


def add_tokens(loads, source, target, first):
    return [
        loads.add(source.at[pl.ds(r, n), :], target.at[pl.ds(r, n), :])
        for r, n in ((0, first), (first, ROWS - first))
    ]


def add_qkv_weights(loads, w_qkv, wq):
    return [
        loads.add(w_qkv.at[:, pl.ds(c, n)], wq.at[:, pl.ds(c, n)]) for c, n in QKV_PIECES
    ]


def project_rows(norm, loads, tokens, weights, product, size):
    blocks = list(range(0, ROWS, size))
    loads.wait(tokens[0])
    norm(0)
    for at in tokens[1:]:
        loads.wait(at)
    loads.wait(weights[0])
    for r in blocks:
        product(r, 0, size)
        if r + size < ROWS:
            norm(r + size)
    for group in QKV_GROUPS:
        for j in group:
            loads.wait(weights[j])
        for j in group:
            for r in range(0, ROWS, STEP):
                product(r, j, STEP)


def spatial_kernel(
    frame, clip, modulation, w_qkv, w_out, out, rows6, x, wq, wo, mod, qkv, att, res, sems, sent
):
    loads = Loads(sems)
    first = loads.add(modulation, rows6)
    tokens = add_tokens(loads, clip.at[frame], x, FRONT)
    weights = add_qkv_weights(loads, w_qkv, wq)
    last = loads.add(w_out, wo)
    loads.start(DEPTH)
    loads.wait(first)
    shift, gain, gate = rows6[0:1, :], 1.0 + rows6[1:2, :], rows6[2:3, :]

    def norm(r):
        modulate(x, mod, shift, gain, slice(r, r + FRONT))

    def product(r, j, size):
        c, n = QKV_PIECES[j]
        qkv[r : r + size, c : c + n] = project(mod[r : r + size, :], wq, (c, n))

    project_rows(norm, loads, tokens, weights, product, FRONT)
    loads.wait(last)
    done = []
    for i, r in enumerate(range(0, ROWS, STEP)):

        def load(which, c):
            rows = slice(r, r + STEP) if which == 0 else slice(0, ROWS)
            return qkv[rows, which * D + c : which * D + c + WIN]

        def store(c, part):
            att[r : r + STEP, c : c + 128] = part

        attend(load, store)
        finish(x, att[r : r + STEP, :], wo, gate, res, slice(r, r + STEP))
        done.append(
            pltpu.make_async_copy(
                res.at[pl.ds(r, STEP), :], out.at[pl.ds(r, STEP), :], sent.at[i]
            )
        )
        done[-1].start()
    for copy in done:
        copy.wait()


def call(kernel, name, out_shape, operands, scratch, copies_in, copies_out, flops, exps):
    anywhere = pl.BlockSpec(memory_space=pl.ANY)
    return pl.pallas_call(
        kernel,
        out_shape=out_shape,
        in_specs=[anywhere] * len(operands),
        out_specs=anywhere,
        scratch_shapes=scratch
        + [pltpu.SemaphoreType.DMA((copies_in,)), pltpu.SemaphoreType.DMA((copies_out,))],
        compiler_params=pltpu.CompilerParams(vmem_limit_bytes=VMEM_BYTES),
        cost_estimate=pl.CostEstimate(
            flops=flops, bytes_accessed=15 * 10**6, transcendentals=exps
        ),
        name=name,
    )(*operands)


def buffer(*shape):
    return pltpu.VMEM(shape, jnp.bfloat16)


def spatial(clip, modulation, w_qkv, w_out, frame):
    def kernel(*refs):
        spatial_kernel(frame, *refs)

    return call(
        kernel,
        "spatial%d" % frame,
        jax.ShapeDtypeStruct((ROWS, D), jnp.bfloat16),
        (clip, modulation, w_qkv, w_out),
        [
            pltpu.VMEM((6, D), jnp.float32),
            buffer(ROWS, D),
            buffer(D, 3 * D),
            buffer(D, D),
            buffer(ROWS, D),
            buffer(ROWS, 3 * D),
            buffer(ROWS, D),
            buffer(ROWS, D),
        ],
        1 + ROWS // STEP + len(QKV_PIECES) + 1,
        ROWS // STEP,
        8 * 10**9,
        4 * 10**6,
    )


def permutation():
    row = lax.broadcasted_iota(jnp.int32, (BLOCK, BLOCK), 0)
    col = lax.broadcasted_iota(jnp.int32, (BLOCK, BLOCK), 1)
    swap = ((row & 15) == (col >> 4)) & ((row >> 4) == (col & 15))
    return swap.astype(jnp.float32).astype(jnp.bfloat16)


def move(swap, rows):
    return jnp.dot(swap, rows, preferred_element_type=jnp.float32).astype(jnp.bfloat16)


def temporal_project(x, mod, moved, wq, swap, shift, gain, loads, tokens, weights, put):
    def norm(r):
        modulate(x, mod, shift, gain, slice(r, r + STEP))
        moved[r : r + STEP, :] = move(swap, mod[r : r + STEP, :])

    def product(r, j, size):
        c, n = QKV_PIECES[j]
        put(r // STEP, c, n, project(moved[r : r + STEP, :], wq, (c, n)))

    project_rows(norm, loads, tokens, weights, product, STEP)


def temporal_in_kernel(
    tokens0, modulation, w_qkv, qkv_out, rows6, x, wq, mod, moved, qkv, sems, sent
):
    loads = Loads(sems)
    first = loads.add(modulation, rows6)
    tokens = add_tokens(loads, tokens0, x, STEP)
    weights = add_qkv_weights(loads, w_qkv, wq)
    loads.start(DEPTH)
    loads.wait(first)
    done = []

    def put(g, c, n, part):
        qkv[:, g * QUARTER : (g + 1) * QUARTER, c : c + n] = part.reshape(PAIRS, QUARTER, n)
        if g == 1:
            done.append(
                pltpu.make_async_copy(
                    qkv.at[:, :, pl.ds(c, n)], qkv_out.at[:, :, pl.ds(c, n)], sent.at[len(done)]
                )
            )
            done[-1].start()

    temporal_project(
        x, mod, moved, wq, permutation(), rows6[3:4, :], 1.0 + rows6[4:5, :], loads, tokens, weights, put
    )
    for copy in done:
        copy.wait()


def temporal_in(tokens0, modulation, w_qkv):
    return call(
        temporal_in_kernel,
        "temporal_in",
        jax.ShapeDtypeStruct((PAIRS, 2 * QUARTER, 3 * D), jnp.bfloat16),
        (tokens0, modulation, w_qkv),
        [
            pltpu.VMEM((6, D), jnp.float32),
            buffer(ROWS, D),
            buffer(D, 3 * D),
            buffer(ROWS, D),
            buffer(ROWS, D),
            buffer(PAIRS, 2 * QUARTER, 3 * D),
        ],
        1 + ROWS // STEP + len(QKV_PIECES),
        len(QKV_PIECES),
        5 * 10**9,
        1000,
    )


def temporal_out_kernel(
    tokens1, tokens0, qkv0, modulation, w_qkv, w_out, out,
    rows6, x1, x0, wq, wo, mod, moved, qkv, att, res, sems, sent,
):
    loads = Loads(sems)
    first = loads.add(modulation, rows6)
    tokens = add_tokens(loads, tokens1, x1, STEP)
    weights = add_qkv_weights(loads, w_qkv, wq)
    early = loads.add(qkv0, qkv.at[:, pl.ds(0, 2 * QUARTER), :])
    last = [loads.add(w_out, wo), loads.add(tokens0, x0)]
    loads.start(DEPTH)
    loads.wait(first)
    swap = permutation()

    def put(g, c, n, part):
        at = (2 + g) * QUARTER
        qkv[:, at : at + QUARTER, c : c + n] = part.reshape(PAIRS, QUARTER, n)

    temporal_project(
        x1, mod, moved, wq, swap, rows6[3:4, :], 1.0 + rows6[4:5, :], loads, tokens, weights, put
    )
    loads.wait(early)
    keep = (lax.broadcasted_iota(jnp.int32, (PAIR, PAIR), 0) // 16 % 2) == (
        lax.broadcasted_iota(jnp.int32, (PAIR, PAIR), 1) // 16 % 2
    )

    def one_pair(i):
        def load(which, c):
            return qkv[i, :, which * D + c : which * D + c + WIN]

        def store(c, part):
            rows = slice(i * QUARTER, (i + 1) * QUARTER)
            for k in range(4):
                att[k, rows, c : c + 128] = part[k * QUARTER : (k + 1) * QUARTER]

        attend(load, store, keep)

    for i in range(PAIRS):
        one_pair(i)
    for at in last:
        loads.wait(at)
    done = []
    for k in range(4):
        f, g = k // 2, k % 2
        back = move(swap, att[k])
        rows = slice(g * BLOCK, (g + 1) * BLOCK)
        finish((x0, x1)[f], back, wo, rows6[5:6, :], res.at[f], rows)
        for a in range(16):
            done.append(
                pltpu.make_async_copy(
                    res.at[f, pl.ds(g * BLOCK + a * 16, 16), :], out.at[g * 16 + a, f], sent.at[k * 16 + a]
                )
            )
            done[-1].start()
    for copy in done:
        copy.wait()


def temporal_out(tokens1, tokens0, qkv0, modulation, w_qkv, w_out):
    return call(
        temporal_out_kernel,
        "temporal_out",
        jax.ShapeDtypeStruct((SEQ, 2, PATCHES, D), jnp.bfloat16),
        (tokens1, tokens0, qkv0, modulation, w_qkv, w_out),
        [
            pltpu.VMEM((6, D), jnp.float32),
            buffer(ROWS, D),
            buffer(ROWS, D),
            buffer(D, 3 * D),
            buffer(D, D),
            buffer(ROWS, D),
            buffer(ROWS, D),
            buffer(PAIRS, PAIR, 3 * D),
            buffer(4, BLOCK, D),
            buffer(2, ROWS, D),
        ],
        1 + ROWS // STEP + len(QKV_PIECES) + 3,
        64,
        8 * 10**9,
        2 * 10**6,
    )


def exchange(x):
    return lax.all_to_all(x, "seq", split_axis=0, concat_axis=0, tiled=True)


def body(clip, modulation, w_qkv_s, w_out_s, w_qkv_t, w_out_t):
    got = []
    for frame in range(2):
        sent = spatial(clip, modulation, w_qkv_s, w_out_s, frame)
        got.append(exchange(sent.reshape(SEQ, PATCHES, D)).reshape(ROWS, D))
    qkv0 = temporal_in(got[0], modulation, w_qkv_t)
    result = temporal_out(got[1], got[0], qkv0, modulation, w_qkv_t, w_out_t)
    back = exchange(result)
    return jnp.swapaxes(back, 0, 1).reshape(2, P_SIZE, D)


def solution(mesh):
    return jax.shard_map(
        body,
        mesh=mesh,
        in_specs=(P(("dp", "seq"), None, None), P("dp", None), P(), P(), P(), P()),
        out_specs=P(("dp", "seq"), None, None),
        check_vma=False,
    )
```
